32 devices in a mesh: chan: 2 (over x), grid: 8 (over z, core), vis: 2 (over y).
Axes of the slice: x: 2, y: 2, z: 4, core: 2. Of those that a mesh axis runs over, the one named last changes fastest.
Arguments:
- model_grid: bfloat16 [4, 1024, 8192], P('chan', 'grid'), parts along dimension 0, may hold values from -6 to 6
- kernels: float32 [32, 28], replicated, may hold values from -1.5 to 1.5
- cover: int32 [4, 32], P(('chan', 'vis')), parts along dimension 0, may hold values from 0 to 511, as said below
- cells: int32 [4, 32, 6144], P(('chan', 'vis'), None, 'grid'), parts along dimension 0, may hold values from 0 to 15609, as said below
- planes: int32 [4, 32, 6144], P(('chan', 'vis'), None, 'grid'), parts along dimension 0, may hold values from 0 to 31
- observed: float32 [4, 2, 32, 6144], P('chan', 'vis', None, 'grid'), parts along dimension 0, may hold values from -6 to 6
- weights: float32 [4, 32, 6144], P(('chan', 'vis'), None, 'grid'), parts along dimension 0, may hold values from 0.2 to 2
Outputs:
- residual_grid: float32 [4, 1024, 8192], P('chan', 'grid', 'vis'), parts along dimension 0
The draws below stay inside these ranges and needn't reach their ends.
There are 2 independent parts, one for each index of `chan`. The reference program is written for one: setup_inputs(seed, part) draws one part's arguments, and reference() takes and returns one part's arrays. A program takes and returns all parts, laid end to end along the dimension named above; an argument that names none is the same for every part. Nothing has to cross between parts.
Inputs may be any that keep to these rules, and one draw needn't show every extreme that they name: `cover`: each row lists 32 different patch numbers below 512; patch p lies in grid rows (p // 64) * 128 onward, the tile of one grid device. In every row, 2 tiles hold exactly 8 listed patches, 4 tiles hold 4 and the others none; which tiles, and the order of the list, vary from row to row. cells = r * 128 + c with 0 <= r <= 121 and 0 <= c <= 121, so that every kernel lies inside its patch.
All inputs are finite; a program needn't handle non-finite values.
Results may differ from the reference program's by a relative error of at most 0.0043.
Values may be sent and summed in bfloat16 or wider, within the bound.
No kernel may reach another device: no remote copies, remote signals or barrier semaphores. Data moves between devices by JAX's collectives and lax.ppermute only.
A program may use at most 64 MiB of HBM per device.

```python
import math
import jax
import jax.numpy as jnp
import numpy as np
from jax import lax

NV = 8192
PH = 128
PW = 128
KS = 7
WPLANES = 32
COVER = 32
NU = 1024
PPT = 64
CAP = 8
SLOTS = 6144
N_GRID = 8
N_VIS = 2


def draw_cover(key, part):
    key = jax.random.fold_in(key, 11)
    quarter = N_GRID // 4
    counts = [CAP] * quarter + [CAP // 2] * (2 * quarter) + [0] * (N_GRID - 3 * quarter)
    position = np.repeat(np.arange(N_GRID), counts).astype(np.int32)
    slot_rank = np.concatenate([np.arange(amount, dtype=np.int32) for amount in counts]).astype(np.int32)

    def one_block(block_key):
        owner_key, column_key = jax.random.split(block_key)
        owner_order = jax.random.permutation(owner_key, N_GRID)
        column_keys = jax.random.split(column_key, N_GRID)
        column_orders = jax.vmap(lambda single: jax.random.permutation(single, PPT))(column_keys)
        chosen_owner = owner_order[position]
        chosen_column = column_orders[position, slot_rank]
        return (chosen_owner * PPT + chosen_column).astype(jnp.int32)
    return jax.vmap(one_block)(jax.random.split(key, N_VIS))


def draw_cells(key, part):
    key = jax.random.fold_in(key, 23)
    row_key, column_key = jax.random.split(key)
    shape = (N_VIS, COVER, SLOTS)
    row_pick = jax.random.randint(row_key, shape, 0, PH - KS + 1)
    column_pick = jax.random.randint(column_key, shape, 0, PW - KS + 1)
    return (row_pick * PW + column_pick).astype(jnp.int32)


def plant(drawn, own_key, smallest, top_value):
    dims = drawn.shape
    spot = [jax.random.randint(jax.random.fold_in(own_key, axis), (), 0, dims[axis]) for axis in range(len(dims))]
    drawn = drawn.at[tuple(spot)].set(smallest)
    longest = dims.index(max(dims))
    spot[longest] = (spot[longest] + 1) % dims[longest]
    return drawn.at[tuple(spot)].set(top_value)


def block_levels(own_key, shape, pieces, smallest, high):
    gain, own = 1.0, jax.random.fold_in(own_key, 6)
    for dim, blocks in pieces:
        heights = jnp.exp(jax.random.uniform(jax.random.fold_in(own, dim), (blocks,), jnp.float32, smallest / len(pieces), high / len(pieces)))
        gain = gain * jnp.repeat(heights, shape[dim] // blocks).reshape([-1 if axis == dim else 1 for axis in range(len(shape))])
    return gain


def normal_values(stream_key, shape, width, most, cuts=(), kind=jnp.bfloat16):
    level = block_levels(stream_key, shape, cuts, -0.22, 0.18) if cuts else 1.0
    array = jax.random.normal(stream_key, shape, jnp.float32) * width * level
    return jnp.minimum(jnp.maximum(array, -most), most).astype(kind)


def setup_inputs(seed: int = 0, part: int = 0) -> dict:
    splits = jax.random.split(jax.random.key(seed), 8)
    part_splits = jax.random.split(jax.random.fold_in(splits[7], part), 8)
    return {
        "model_grid": normal_values(part_splits[0], (2, NU, NV), 1.0, 6.0, ((1, 8),)),
        "kernels": normal_values(splits[1], (WPLANES, 4 * KS), (2 * KS) ** -0.5, 1.5, (), jnp.float32),
        "cover": draw_cover(jax.random.fold_in(jax.random.fold_in(splits[7], part), 71), part),
        "cells": draw_cells(jax.random.fold_in(jax.random.fold_in(splits[7], part), 71), part),
        "planes": plant(jax.random.randint(part_splits[4], (N_VIS, COVER, SLOTS), 0, WPLANES), jax.random.fold_in(part_splits[4], 1), 0, WPLANES - 1).astype(jnp.int32),
        "observed": normal_values(part_splits[5], (2, N_VIS, COVER, SLOTS), 1.0, 6.0, ((1, 2), (3, 8)), jnp.float32),
        "weights": jnp.clip(jnp.exp(math.log(2.0) - 2.3025851 * jax.random.uniform(part_splits[6], (N_VIS, COVER, SLOTS), jnp.float32) ** block_levels(part_splits[6], (N_VIS, COVER, SLOTS), ((0, 2), (2, 8)), -0.2, 0.2)), 0.2, 2.0),
    }


def residual_patch(patch_cells, observed_pair, weight_row, cell_row, plane_row, kernels):
    rows_in = patch_cells.shape[1]
    cols_in = patch_cells.shape[2]
    support = kernels.shape[1] // 4
    planes_all = kernels.shape[0]
    count_rows = cell_row.shape[0]
    row_off = cell_row // cols_in
    col_off = cell_row % cols_in
    plane_hot = (plane_row[:, None] == jnp.arange(planes_all, dtype=jnp.int32)[None, :]).astype(jnp.float32)
    taps = jnp.dot(plane_hot, kernels, precision=lax.Precision.HIGHEST)
    u_dist = jnp.arange(rows_in, dtype=jnp.int32)[None, :] - row_off[:, None]
    v_dist = jnp.arange(cols_in, dtype=jnp.int32)[None, :] - col_off[:, None]
    u_real = jnp.zeros((count_rows, rows_in), jnp.float32)
    u_imag = jnp.zeros((count_rows, rows_in), jnp.float32)
    v_real = jnp.zeros((count_rows, cols_in), jnp.float32)
    v_imag = jnp.zeros((count_rows, cols_in), jnp.float32)
    for offset in range(support):
        u_hit = u_dist == offset
        v_hit = v_dist == offset
        u_real = u_real + jnp.where(u_hit, taps[:, offset:offset + 1], 0.0)
        u_imag = u_imag + jnp.where(u_hit, taps[:, support + offset:support + offset + 1], 0.0)
        v_real = v_real + jnp.where(v_hit, taps[:, 2 * support + offset:2 * support + offset + 1], 0.0)
        v_imag = v_imag + jnp.where(v_hit, taps[:, 3 * support + offset:3 * support + offset + 1], 0.0)
    u_rows = jnp.concatenate([u_real, u_imag], axis=1).astype(jnp.bfloat16)
    real_part = patch_cells[0]
    imag_part = patch_cells[1]
    upper = jnp.concatenate([real_part, imag_part], axis=1)
    lower = jnp.concatenate([-imag_part, real_part], axis=1)
    w_matrix = jnp.concatenate([upper, lower], axis=0)
    product = jnp.dot(u_rows, w_matrix, preferred_element_type=jnp.float32)
    m_real = product[:, :cols_in]
    m_imag = product[:, cols_in:]
    model_re = jnp.sum(m_real * v_real - m_imag * v_imag, axis=1)
    model_im = jnp.sum(m_real * v_imag + m_imag * v_real, axis=1)
    res_re = weight_row * (observed_pair[0] - model_re)
    res_im = weight_row * (observed_pair[1] - model_im)
    s_real = res_re[:, None] * v_real + res_im[:, None] * v_imag
    s_imag = res_im[:, None] * v_real - res_re[:, None] * v_imag
    s_rows = jnp.concatenate([s_real, s_imag], axis=1).astype(jnp.bfloat16)
    q_matrix = jnp.dot(u_rows.T, s_rows, preferred_element_type=jnp.float32)
    q_real = q_matrix[:rows_in, :cols_in] + q_matrix[rows_in:, cols_in:]
    q_imag = q_matrix[:rows_in, cols_in:] - q_matrix[rows_in:, :cols_in]
    return jnp.stack([q_real, q_imag])


def reference(model_grid, kernels, cover, cells, planes, observed, weights):
    grid_rows = model_grid.shape[1]
    grid_cols = model_grid.shape[2]
    per_tile = grid_cols // PW
    entries = cover.shape[0] * cover.shape[1]
    slot_count = cells.shape[2]
    flat_cover = cover.reshape(entries).astype(jnp.int32)
    flat_cells = cells.reshape(entries, slot_count)
    flat_planes = planes.reshape(entries, slot_count)
    flat_observed = jnp.transpose(observed, (1, 2, 0, 3)).reshape(entries, 2, slot_count)
    flat_weights = weights.reshape(entries, slot_count)

    def add_entry(summed, item):
        patch_id, cell_row, plane_row, observed_pair, weight_row = item
        row_start = ((patch_id // per_tile) * PH).astype(jnp.int32)
        col_start = ((patch_id % per_tile) * PW).astype(jnp.int32)
        zero_index = jnp.zeros((), jnp.int32)
        patch_cells = lax.dynamic_slice(model_grid, (zero_index, row_start, col_start), (2, PH, PW))
        q_patch = residual_patch(patch_cells, observed_pair, weight_row, cell_row, plane_row, kernels)
        current = lax.dynamic_slice(summed, (zero_index, row_start, col_start), (2, PH, PW))
        summed = lax.dynamic_update_slice(summed, current + q_patch, (zero_index, row_start, col_start))
        return summed, None

    start = jnp.zeros((2, grid_rows, grid_cols), jnp.float32)
    summed, _ = lax.scan(add_entry, start, (flat_cover, flat_cells, flat_planes, flat_observed, flat_weights))
    return summed
```

```python
import functools

import jax
import jax.numpy as jnp
from jax import lax
from jax.experimental import pallas as pl
from jax.experimental.pallas import tpu as pltpu
from jax.sharding import PartitionSpec as P

PW = 128
LANES = 128
FIELDS = 6
BF16 = jnp.bfloat16
F32 = jnp.float32
I32 = jnp.int32
VMEM_LIMIT = 48 * 1024 * 1024
EMPTY = 255


def round_up(value, unit):
    return -(-value // unit) * unit


def iota(shape, dim):
    return lax.broadcasted_iota(I32, shape, dim)


def pack_kernel(
    place_ref, cover_ref, cells_ref, planes_ref, observed_ref, weights_ref,
    *refs, count, tiles, per_tile, per_slab, capacity, rows,
):
    info_ref = refs[0]
    outs = refs[1:]
    me = place_ref[0]
    slab = place_ref[1]
    cover_row = cover_ref[...]
    across = jnp.broadcast_to(cover_row, (count, count))
    left = iota((count, count), 0)
    right = iota((count, count), 1)
    cover_col = jnp.sum(jnp.where(left == right, across, 0), axis=1, keepdims=True)

    def order_key(patch, entry):
        owner = patch // per_tile
        foreign = jnp.where((patch - owner * per_tile) // per_slab == slab, 1, 0)
        return owner, foreign * count + entry

    owner_i, key_i = order_key(cover_col, iota((count, 1), 0))
    owner_j, key_j = order_key(cover_row, iota((1, count), 1))
    same = owner_i == owner_j
    rank_row = jnp.sum(jnp.where(same & (key_i < key_j), 1, 0), axis=0, keepdims=True)
    rank_col = jnp.sum(jnp.where(same & (key_j < key_i), 1, 0), axis=1, keepdims=True)

    slot = iota((count, LANES), 1)
    own = (owner_i == me) & (rank_col == slot)
    column = cover_col - owner_i * per_tile
    listed = jnp.sum(jnp.where(own, column + 1, 0), axis=0, keepdims=True)
    total = jnp.sum(jnp.where(owner_i == me, 1, 0), axis=0, keepdims=True)
    lane = iota((1, LANES), 1)
    info = jnp.where(lane < capacity, listed - 1, jnp.where(lane == capacity, total, 0))
    info_ref[...] = jnp.broadcast_to(info, info_ref.shape)

    route = (owner_j ^ me) * capacity + rank_row
    spread = (iota((count, FIELDS * count), 1) % count == iota((count, FIELDS * count), 0)).astype(F32)
    wide = jnp.dot(
        jnp.broadcast_to(route.astype(F32), (8, count)).astype(BF16), spread.astype(BF16),
        preferred_element_type=F32,
    )[0:1].astype(I32)
    field_j = iota((1, FIELDS * count), 1) // count

    cells = cells_ref[0]
    row_off = cells // PW
    data = jnp.concatenate(
        [
            row_off.astype(F32).astype(BF16),
            (cells - row_off * PW).astype(F32).astype(BF16),
            planes_ref[0].astype(F32).astype(BF16),
            observed_ref[0, 0].astype(BF16),
            observed_ref[1, 0].astype(BF16),
            weights_ref[0].astype(BF16),
        ],
        axis=0,
    )
    line = iota((rows, FIELDS * count), 0)
    for m in range(tiles):
        field_i = line // capacity
        pick = (field_i == field_j) & (wide == m * capacity + line - field_i * capacity)
        block = jnp.dot(pick.astype(F32).astype(BF16), data, preferred_element_type=F32)
        outs[m][...] = block.astype(BF16)


def pack(place, cover, cells, planes, observed, weights, tiles, per_tile, per_slab):
    count, slots = cells.shape[1:]
    capacity = 2 * count // tiles
    rows = round_up(FIELDS * capacity, 16)
    whole = lambda shape: pl.BlockSpec(shape, lambda i, p: (0,) * len(shape))
    return pl.pallas_call(
        functools.partial(
            pack_kernel, count=count, tiles=tiles, per_tile=per_tile, per_slab=per_slab,
            capacity=capacity, rows=rows,
        ),
        grid_spec=pltpu.PrefetchScalarGridSpec(
            num_scalar_prefetch=1,
            grid=(1,),
            in_specs=[whole(a.shape) for a in (cover, cells, planes, observed, weights)],
            out_specs=[whole((8, LANES))] + [whole((rows, slots))] * tiles,
        ),
        out_shape=[jax.ShapeDtypeStruct((8, LANES), I32)]
        + [jax.ShapeDtypeStruct((rows, slots), BF16)] * tiles,
        compiler_params=pltpu.CompilerParams(vmem_limit_bytes=VMEM_LIMIT),
        name="pack_by_tile",
    )(place, cover, cells, planes, observed, weights)


def fill_tables(kern_ref, wide_ref, table_ref, support):
    wide_ref[...] = jnp.zeros_like(wide_ref)
    wide_ref[0 : kern_ref.shape[0], 0 : kern_ref.shape[1]] = kern_ref[...]
    flipped = wide_ref[...].T
    zero = jnp.zeros((8 - support, LANES), F32)
    for group in range(4):
        taps = flipped[support * group : support * (group + 1)]
        table_ref[group] = jnp.concatenate([taps, zero], axis=0)


def pick(array, index, axis):
    return jnp.take_along_axis(array, index, axis=axis)


def tap_places(offset):
    wide = jnp.broadcast_to(offset, (16, LANES))
    s = iota((16, LANES), 0)
    return jnp.minimum((s - wide) & 15, 7), (wide + 15 - s) >> 4


def wrapped(taps, places):
    return jnp.concatenate([pick(taps, places[0:8], 0), pick(taps, places[8:16], 0)], axis=0)


def expand(ref, base, cols, rows, group):
    group = group.astype(F32).astype(BF16)
    for q in range(PW // 16):
        ref[base + 16 * q : base + 16 * q + 16, cols] = jnp.where(group == BF16(q), rows, BF16(0))


def degrid_start(f_ref, item, table_ref, wt_ref, u_ref, m_ref, v_ref, g_ref):
    for t in range(u_ref.shape[1] // LANES):
        cols = pl.ds(t * LANES, LANES)
        row_off = f_ref[item, 0:1, cols].astype(I32)
        col_off = f_ref[item, 1:2, cols].astype(I32)
        plane = jnp.broadcast_to(f_ref[item, 2:3, cols].astype(I32), (8, LANES))
        u_place, u_group = tap_places(row_off)
        v_place, v_group = tap_places(col_off)
        u_re = wrapped(pick(table_ref[0], plane, 1), u_place).astype(BF16)
        u_im = wrapped(pick(table_ref[1], plane, 1), u_place).astype(BF16)
        v_ref[0, :, cols] = wrapped(pick(table_ref[2], plane, 1), v_place)
        v_ref[1, :, cols] = wrapped(pick(table_ref[3], plane, 1), v_place)
        g_ref[:, cols] = v_group
        expand(u_ref, 0, cols, u_re, u_group)
        expand(u_ref, PW, cols, u_im, u_group)
    m_ref[...] = jnp.dot(wt_ref[...], u_ref[...], preferred_element_type=F32)


def degrid_end(f_ref, item, u_ref, m_ref, s_ref, v_ref, g_ref, q_ref):
    for t in range(u_ref.shape[1] // LANES):
        cols = pl.ds(t * LANES, LANES)
        group = g_ref[:, cols]
        m_re = jnp.zeros((16, LANES), F32)
        m_im = jnp.zeros((16, LANES), F32)
        for q in range(PW // 16):
            hit = group == q
            m_re = jnp.where(hit, m_ref[16 * q : 16 * q + 16, cols], m_re)
            m_im = jnp.where(hit, m_ref[PW + 16 * q : PW + 16 * q + 16, cols], m_im)
        v_re = v_ref[0, :, cols]
        v_im = v_ref[1, :, cols]
        model_re = jnp.sum(m_re * v_re - m_im * v_im, axis=0, keepdims=True)
        model_im = jnp.sum(m_re * v_im + m_im * v_re, axis=0, keepdims=True)
        weight = f_ref[item, 5:6, cols]
        res_re = weight * (f_ref[item, 3:4, cols] - model_re)
        res_im = weight * (f_ref[item, 4:5, cols] - model_im)
        s_re = (res_re * v_re + res_im * v_im).astype(BF16)
        s_im = (res_im * v_re - res_re * v_im).astype(BF16)
        expand(s_ref, 0, cols, s_re, group)
        expand(s_ref, PW, cols, s_im, group)
    q_ref[...] += lax.dot_general(
        u_ref[...], s_ref[...], (((1,), (1,)), ((), ())), preferred_element_type=F32
    )


def residual_kernel(info_ref, *refs, blocks, capacity, support):
    block_refs = refs[:blocks]
    model_ref, kern_ref, patch_ref, send_ref = refs[blocks : blocks + 4]
    f_ref, table_ref, wide_ref, wt_ref, u_ref, m_ref, s_ref, v_ref, g_ref, q_ref = refs[blocks + 4 :]
    k = pl.program_id(0)

    @pl.when(k == 0)
    def _():
        fill_tables(kern_ref, wide_ref, table_ref, support)
        shape = (8 * capacity, block_refs[0].shape[0])
        line = iota(shape, 0)
        order = (iota(shape, 1) == (line & 7) * capacity + (line >> 3)).astype(F32).astype(BF16)
        for b in range(blocks):
            fields = jnp.dot(order, block_refs[b][...], preferred_element_type=F32)
            for slot in range(capacity):
                f_ref[b * capacity + slot] = fields[8 * slot : 8 * slot + 8]

    @pl.when(k < info_ref[0, capacity])
    def _():
        real = model_ref[0].T
        imag = model_ref[1].T
        wt_ref[0:PW, 0:PW] = real
        wt_ref[0:PW, PW:] = -imag
        wt_ref[PW:, 0:PW] = imag
        wt_ref[PW:, PW:] = real
        q_ref[...] = jnp.zeros_like(q_ref)

        def start(b, i):
            degrid_start(
                f_ref, b * capacity + k, table_ref, wt_ref, u_ref.at[i], m_ref.at[i], v_ref.at[i], g_ref.at[i]
            )

        def end(b, i):
            degrid_end(
                f_ref, b * capacity + k, u_ref.at[i], m_ref.at[i], s_ref, v_ref.at[i], g_ref.at[i], q_ref
            )

        start(0, 0)

        def step(j, carry):
            b = 2 * j
            end(b, 0)
            start(b + 1, 1)
            end(b + 1, 1)
            start(jnp.minimum(b + 2, blocks - 1), 0)
            return carry

        lax.fori_loop(0, blocks // 2, step, 0)
        q_re = q_ref[0:PW, 0:PW] + q_ref[PW:, PW:]
        q_im = q_ref[0:PW, PW:] - q_ref[PW:, 0:PW]
        patch_ref[0] = q_re
        patch_ref[1] = q_im
        send_ref[0:PW] = q_re.astype(BF16)
        send_ref[PW : 2 * PW] = q_im.astype(BF16)

    column = jnp.where(k < info_ref[0, capacity], info_ref[0, k], EMPTY)
    send_ref[2 * PW :] = jnp.full((16, PW), column, I32).astype(F32).astype(BF16)


def residual(info, blocks, model_grid, kernels, capacity):
    rows, slots = blocks[0].shape
    patch_rows = model_grid.shape[1]
    whole = lambda shape: pl.BlockSpec(shape, lambda k, i: (0,) * len(shape))
    return pl.pallas_call(
        functools.partial(
            residual_kernel, blocks=len(blocks), capacity=capacity, support=kernels.shape[1] // 4
        ),
        grid_spec=pltpu.PrefetchScalarGridSpec(
            num_scalar_prefetch=1,
            grid=(capacity,),
            in_specs=[whole((rows, slots))] * len(blocks)
            + [
                pl.BlockSpec((2, patch_rows, PW), lambda k, i: (0, 0, jnp.maximum(i[0, k], 0))),
                whole(kernels.shape),
            ],
            out_specs=[
                pl.BlockSpec((None, 2, patch_rows, PW), lambda k, i: (k, 0, 0, 0)),
                pl.BlockSpec((None, 2 * PW + 16, PW), lambda k, i: (k, 0, 0)),
            ],
            scratch_shapes=[
                pltpu.VMEM((len(blocks) * capacity, 8, slots), F32),
                pltpu.VMEM((4, 8, LANES), F32),
                pltpu.VMEM((LANES, LANES), F32),
                pltpu.VMEM((2 * PW, 2 * PW), BF16),
                pltpu.VMEM((2, 2 * PW, slots), BF16),
                pltpu.VMEM((2, 2 * PW, slots), F32),
                pltpu.VMEM((2 * PW, slots), BF16),
                pltpu.VMEM((2, 2, 16, slots), F32),
                pltpu.VMEM((2, 16, slots), I32),
                pltpu.VMEM((2 * PW, 2 * PW), F32),
            ],
        ),
        out_shape=[
            jax.ShapeDtypeStruct((capacity, 2, patch_rows, PW), F32),
            jax.ShapeDtypeStruct((capacity, 2 * PW + 16, PW), BF16),
        ],
        compiler_params=pltpu.CompilerParams(vmem_limit_bytes=VMEM_LIMIT),
        name="degrid_and_grid",
    )(info, *blocks, model_grid, kernels)


def assemble_kernel(info_ref, place_ref, *refs, others, capacity, per_slab, patches):
    received = refs[:others]
    own_ref, out_ref = refs[others:]
    first = place_ref[1] * per_slab + pl.program_id(0) * patches
    out_ref[...] = jnp.zeros_like(out_ref)

    def add(column, real, imag):
        cols = pl.ds(pl.multiple_of((column - first) * PW, PW), PW)
        out_ref[0, :, cols] += real
        out_ref[1, :, cols] += imag

    def add_own(k, carry):
        column = info_ref[0, k]

        @pl.when((k < info_ref[0, capacity]) & (column >= first) & (column < first + patches))
        def _():
            add(column, own_ref[k, 0], own_ref[k, 1])

        return carry

    lax.fori_loop(0, capacity, add_own, 0)
    for ref in received:

        def add_received(k, carry):
            column = jnp.max(ref[k, 2 * PW :].astype(F32)).astype(I32)

            @pl.when((column >= first) & (column < first + patches))
            def _():
                add(column, ref[k, 0:PW].astype(F32), ref[k, PW : 2 * PW].astype(F32))

            return carry

        lax.fori_loop(0, capacity, add_received, 0)


def assemble(info, place, received, own, per_slab):
    capacity, _, patch_rows, _ = own.shape
    patches = min(per_slab, 8)
    whole = lambda shape: pl.BlockSpec(shape, lambda j, i, p: (0,) * len(shape))
    return pl.pallas_call(
        functools.partial(
            assemble_kernel, others=len(received), capacity=capacity, per_slab=per_slab, patches=patches
        ),
        grid_spec=pltpu.PrefetchScalarGridSpec(
            num_scalar_prefetch=2,
            grid=(per_slab // patches,),
            in_specs=[whole(a.shape) for a in (*received, own)],
            out_specs=pl.BlockSpec((2, patch_rows, patches * PW), lambda j, i, p: (0, 0, j)),
        ),
        out_shape=jax.ShapeDtypeStruct((2, patch_rows, per_slab * PW), F32),
        compiler_params=pltpu.CompilerParams(vmem_limit_bytes=VMEM_LIMIT),
        name="assemble_tile",
    )(info, place, *received, own)


def swap(array, axis, distance):
    size = lax.axis_size(axis)
    return lax.ppermute(array, axis, [(i, i ^ distance) for i in range(size)])


def shards(model_grid, kernels, cover, cells, planes, observed, weights):
    tiles = lax.axis_size("grid")
    slabs = lax.axis_size("vis")
    per_tile = model_grid.shape[2] // PW
    per_slab = per_tile // slabs
    capacity = 2 * cover.shape[1] // tiles
    place = jnp.stack([lax.axis_index("grid"), lax.axis_index("vis")]).astype(I32)
    info, *blocks = pack(place, cover, cells, planes, observed, weights, tiles, per_tile, per_slab)
    arrived = [blocks[0], swap(blocks[1], "grid", 1)]
    across = {m: swap(blocks[m ^ 1], "grid", 1) for m in range(2, tiles, 2)}
    for m in range(tiles - 2, 0, -2):
        arrived += [swap(blocks[m], "grid", m), swap(across[m], "grid", m)]
    own, send = residual(info, arrived, model_grid, kernels, capacity)
    received = [swap(send, "vis", v) for v in range(1, slabs)]
    return assemble(info, place, received, own, per_slab)


def solution(mesh):
    placed = (
        P("chan", "grid", None),
        P(),
        P(("chan", "vis"), None),
        P(("chan", "vis"), None, "grid"),
        P(("chan", "vis"), None, "grid"),
        P("chan", "vis", None, "grid"),
        P(("chan", "vis"), None, "grid"),
    )
    return jax.shard_map(
        shards, mesh=mesh, in_specs=placed, out_specs=P("chan", "grid", "vis"), check_vma=False
    )
```

```python
import functools

import jax
import jax.numpy as jnp
from jax import lax
from jax.experimental import pallas as pl
from jax.experimental.pallas import tpu as pltpu
from jax.sharding import PartitionSpec as P

PW = 128
LANES = 128
FIELDS = 6
BF16 = jnp.bfloat16
F32 = jnp.float32
I32 = jnp.int32
VMEM_LIMIT = 48 * 1024 * 1024
EMPTY = 255


def round_up(value, unit):
    return -(-value // unit) * unit


def whole_block(shape):
    return pl.BlockSpec(shape, lambda *_: (0,) * len(shape))


def iota(shape, dim):
    return lax.broadcasted_iota(I32, shape, dim)


def pack_kernel(
    place_ref, cover_hbm, cells_hbm, planes_hbm, observed_hbm, weights_hbm, info_ref, *refs,
    count, tiles, per_tile, per_slab, capacity, rows,
):
    outs = refs[: tiles // 2]
    cover_ref, cells_ref, planes_ref, observed_ref, weights_ref, sem = refs[tiles // 2 :]
    sources = (cover_hbm, cells_hbm, planes_hbm, observed_hbm, weights_hbm)
    targets = (cover_ref, cells_ref, planes_ref, observed_ref, weights_ref)
    copies = [pltpu.make_async_copy(x, y, sem.at[i]) for i, (x, y) in enumerate(zip(sources, targets))]
    for copy in copies:
        copy.start()
    me = place_ref[0]
    slab = place_ref[1]
    copies[0].wait()
    cover_row = cover_ref[...]
    across = jnp.broadcast_to(cover_row, (count, count))
    left = iota((count, count), 0)
    right = iota((count, count), 1)
    cover_col = jnp.sum(jnp.where(left == right, across, 0), axis=1, keepdims=True)

    def order_key(patch, entry):
        owner = patch // per_tile
        foreign = jnp.where((patch - owner * per_tile) // per_slab == slab, 1, 0)
        return owner, foreign * count + entry

    owner_i, key_i = order_key(cover_col, iota((count, 1), 0))
    owner_j, key_j = order_key(cover_row, iota((1, count), 1))
    same = owner_i == owner_j
    rank_row = jnp.sum(jnp.where(same & (key_i < key_j), 1, 0), axis=0, keepdims=True)
    rank_col = jnp.sum(jnp.where(same & (key_j < key_i), 1, 0), axis=1, keepdims=True)

    slot = iota((count, LANES), 1)
    own = (owner_i == me) & (rank_col == slot)
    column = cover_col - owner_i * per_tile
    listed = jnp.sum(jnp.where(own, column + 1, 0), axis=0, keepdims=True)
    total = jnp.sum(jnp.where(owner_i == me, 1, 0), axis=0, keepdims=True)
    lane = iota((1, LANES), 1)
    info = jnp.where(lane < capacity, listed - 1, jnp.where(lane == capacity, total, 0))
    info_ref[...] = jnp.broadcast_to(info, info_ref.shape)

    route = (owner_j ^ me) * capacity + rank_row
    spread = (iota((count, FIELDS * count), 1) % count == iota((count, FIELDS * count), 0)).astype(F32)
    wide = jnp.dot(
        jnp.broadcast_to(route.astype(F32), (8, count)).astype(BF16), spread.astype(BF16),
        preferred_element_type=F32,
    )[0:1].astype(I32)
    field_j = iota((1, FIELDS * count), 1) // count
    for copy in copies[1:]:
        copy.wait()
    cells = cells_ref[0]
    row_off = cells // PW
    fields = [row_off, cells - row_off * PW, planes_ref[0], observed_ref[0, 0], observed_ref[1, 0], weights_ref[0]]
    data = jnp.concatenate([field.astype(F32).astype(BF16) for field in fields], axis=0)
    line = iota((rows, FIELDS * count), 0)
    for m in range(tiles):
        field_i = line // capacity
        pick = (field_i == field_j) & (wide == m * capacity + line - field_i * capacity)
        block = jnp.dot(pick.astype(F32).astype(BF16), data, preferred_element_type=F32)
        outs[m // 2][rows * (m % 2) : rows * (m % 2 + 1)] = block.astype(BF16)


def in_hbm(array):
    return pltpu.with_memory_space_constraint(array, pltpu.HBM)


def pack(place, cover, cells, planes, observed, weights, tiles, per_tile, per_slab):
    count, slots = cells.shape[1:]
    capacity = 2 * count // tiles
    rows = round_up(FIELDS * capacity, 16)
    arrays = (cover, cells, planes, observed, weights)
    outputs = [((8, LANES), I32)] + [((2 * rows, slots), BF16)] * (tiles // 2)
    return pl.pallas_call(
        functools.partial(
            pack_kernel, count=count, tiles=tiles, per_tile=per_tile, per_slab=per_slab,
            capacity=capacity, rows=rows,
        ),
        grid_spec=pltpu.PrefetchScalarGridSpec(
            num_scalar_prefetch=1,
            grid=(1,),
            in_specs=[pl.BlockSpec(memory_space=pltpu.HBM)] * len(arrays),
            out_specs=[whole_block(shape) for shape, _ in outputs],
            scratch_shapes=[pltpu.VMEM(a.shape, a.dtype) for a in arrays]
            + [pltpu.SemaphoreType.DMA((len(arrays),))],
        ),
        out_shape=[jax.ShapeDtypeStruct(shape, dtype) for shape, dtype in outputs],
        compiler_params=pltpu.CompilerParams(vmem_limit_bytes=VMEM_LIMIT),
        name="pack_by_tile",
    )(place, *[in_hbm(a) for a in arrays])


def fill_tables(kern_ref, wide_ref, table_ref, support):
    wide_ref[...] = jnp.zeros_like(wide_ref)
    wide_ref[0 : kern_ref.shape[0], 0 : kern_ref.shape[1]] = kern_ref[...]
    flipped = wide_ref[...].T
    zero = jnp.zeros((8 - support, LANES), F32)
    for group in range(4):
        taps = flipped[support * group : support * (group + 1)]
        table_ref[group] = jnp.concatenate([taps, zero], axis=0)


def pick(array, index, axis):
    return jnp.take_along_axis(array, index, axis=axis)


def tap_places(offset):
    wide = jnp.broadcast_to(offset, (16, LANES))
    s = iota((16, LANES), 0)
    return jnp.minimum((s - wide) & 15, 7), (wide + 15 - s) >> 4


def wrapped(taps, places):
    return jnp.concatenate([pick(taps, places[0:8], 0), pick(taps, places[8:16], 0)], axis=0)


def expand(ref, base, cols, rows, group):
    group = group.astype(F32).astype(BF16)
    for q in range(PW // 16):
        ref[base + 16 * q : base + 16 * q + 16, cols] = jnp.where(group == BF16(q), rows, BF16(0))


def degrid_start(f_ref, item, table_ref, wt_ref, u_ref, m_ref, v_ref, g_ref):
    for t in range(u_ref.shape[1] // LANES):
        cols = pl.ds(t * LANES, LANES)
        row_off = f_ref[item, 0:1, cols].astype(I32)
        col_off = f_ref[item, 1:2, cols].astype(I32)
        plane = jnp.broadcast_to(f_ref[item, 2:3, cols].astype(I32), (8, LANES))
        u_place, u_group = tap_places(row_off)
        v_place, v_group = tap_places(col_off)
        u_re = wrapped(pick(table_ref[0], plane, 1), u_place).astype(BF16)
        u_im = wrapped(pick(table_ref[1], plane, 1), u_place).astype(BF16)
        v_ref[0, :, cols] = wrapped(pick(table_ref[2], plane, 1), v_place)
        v_ref[1, :, cols] = wrapped(pick(table_ref[3], plane, 1), v_place)
        g_ref[:, cols] = v_group
        expand(u_ref, 0, cols, u_re, u_group)
        expand(u_ref, PW, cols, u_im, u_group)
    m_ref[...] = jnp.dot(wt_ref[...], u_ref[...], preferred_element_type=F32)


def degrid_end(f_ref, item, u_ref, m_ref, s_ref, v_ref, g_ref, q_ref):
    for t in range(u_ref.shape[1] // LANES):
        cols = pl.ds(t * LANES, LANES)
        group = g_ref[:, cols]
        m_re = jnp.zeros((16, LANES), F32)
        m_im = jnp.zeros((16, LANES), F32)
        for q in range(PW // 16):
            hit = group == q
            m_re = jnp.where(hit, m_ref[16 * q : 16 * q + 16, cols], m_re)
            m_im = jnp.where(hit, m_ref[PW + 16 * q : PW + 16 * q + 16, cols], m_im)
        v_re = v_ref[0, :, cols]
        v_im = v_ref[1, :, cols]
        model_re = jnp.sum(m_re * v_re - m_im * v_im, axis=0, keepdims=True)
        model_im = jnp.sum(m_re * v_im + m_im * v_re, axis=0, keepdims=True)
        weight = f_ref[item, 5:6, cols]
        res_re = weight * (f_ref[item, 3:4, cols] - model_re)
        res_im = weight * (f_ref[item, 4:5, cols] - model_im)
        s_re = (res_re * v_re + res_im * v_im).astype(BF16)
        s_im = (res_im * v_re - res_re * v_im).astype(BF16)
        expand(s_ref, 0, cols, s_re, group)
        expand(s_ref, PW, cols, s_im, group)
    q_ref[...] += lax.dot_general(
        u_ref[...], s_ref[...], (((1,), (1,)), ((), ())), preferred_element_type=F32
    )


def residual_kernel(info_ref, *refs, sources, capacity, first, final, resumed, zeros, support):
    refs = list(refs)
    take = lambda number: [refs.pop(0) for _ in range(number)]
    block_refs = take(sources)
    model_ref, kern_ref = take(2)
    before_ref = take(1)[0] if resumed else None
    patch_ref = take(1)[0]
    send_ref = take(1)[0] if final else None
    tile_ref = take(1)[0] if zeros else None
    f_ref, table_ref, wide_ref, wt_ref, wt_next_ref, s_ref, q_ref = take(7)
    u, m, v, g = (take(sources) for _ in range(4))
    step = pl.program_id(0)
    steps = pl.num_programs(0)
    k = first + step - 1
    total = info_ref[0, capacity]
    if zeros:
        zero_ref, sem = take(2)
        width = zero_ref.shape[2]
        clears = [
            pltpu.make_async_copy(zero_ref, tile_ref.at[:, :, pl.ds(i * width, width)], sem.at[i])
            for i in range(zeros)
        ]

    def turn(model, target):
        real = model[0].T
        imag = model[1].T
        target[0:PW, 0:PW] = real
        target[0:PW, PW:] = -imag
        target[PW:, 0:PW] = imag
        target[PW:, PW:] = real

    def start(slot, b, w):
        degrid_start(f_ref, b * capacity + slot, table_ref, w, u[b], m[b], v[b], g[b])

    def end(slot, b):
        degrid_end(f_ref, b * capacity + slot, u[b], m[b], s_ref, v[b], g[b], q_ref)

    @pl.when(step == 0)
    def _():
        if zeros:
            zero_ref[...] = jnp.zeros_like(zero_ref)
            for copy in clears:
                copy.start()
        fill_tables(kern_ref, wide_ref, table_ref, support)
        shape = (8 * capacity, block_refs[0].shape[0])
        line = iota(shape, 0)
        order = (iota(shape, 1) == (line & 7) * capacity + (line >> 3)).astype(F32).astype(BF16)
        for b in range(sources):
            fields = jnp.dot(order, block_refs[b][...], preferred_element_type=F32)
            for slot in range(capacity):
                f_ref[b * capacity + slot] = fields[8 * slot : 8 * slot + 8]
        turn(model_ref, wt_ref)
        start(first, 0, wt_ref)

    @pl.when((step > 0) & (k < total))
    def _():
        turn(model_ref, wt_next_ref)
        q_ref[...] = jnp.zeros_like(q_ref)
        for b in range(sources):
            end(k, b)
            if b + 1 < sources:
                start(k, b + 1, wt_ref)
            else:
                start(jnp.minimum(k + 1, capacity - 1), 0, wt_next_ref)
        wt_ref[...] = wt_next_ref[...]
        q_re = q_ref[0:PW, 0:PW] + q_ref[PW:, PW:]
        q_im = q_ref[0:PW, PW:] - q_ref[PW:, 0:PW]
        if resumed:
            q_re += before_ref[0]
            q_im += before_ref[1]
        patch_ref[0] = q_re
        patch_ref[1] = q_im
        if final:
            send_ref[0:PW] = q_re.astype(BF16)
            send_ref[PW : 2 * PW] = q_im.astype(BF16)

    if final:
        column = jnp.where(k < total, info_ref[0, jnp.maximum(k, 0)], EMPTY)
        send_ref[2 * PW :] = jnp.full((16, PW), column, I32).astype(F32).astype(BF16)
    if zeros:

        @pl.when(step == steps - 1)
        def _():
            for copy in clears:
                copy.wait()


def residual(info, sources, model_grid, kernels, capacity, first, steps, before=None, final=False, tile_columns=0):
    rows, slots = sources[0][0].shape
    rows //= 2
    patch_rows = model_grid.shape[1]
    number = len(sources)
    patch_block = (None, 2, patch_rows, PW)
    in_specs = [pl.BlockSpec((rows, slots), lambda s, i, half=half: (half, 0)) for _, half in sources]
    in_specs += [
        pl.BlockSpec(
            (2, patch_rows, PW), lambda s, i: (0, 0, jnp.maximum(i[0, jnp.minimum(first + s, capacity - 1)], 0))
        ),
        whole_block(kernels.shape),
    ]
    operands = [array for array, _ in sources] + [in_hbm(model_grid), in_hbm(kernels)]
    if before is not None:
        in_specs.append(pl.BlockSpec(patch_block, lambda s, i: (first + jnp.maximum(s - 1, 0), 0, 0, 0)))
        operands.append(before)
    out_specs = [pl.BlockSpec(patch_block, lambda s, i: (jnp.maximum(s - 1, 0), 0, 0, 0))]
    out_shape = [jax.ShapeDtypeStruct((steps, 2, patch_rows, PW), F32)]
    scratch = [
        pltpu.VMEM((number * capacity, 8, slots), F32),
        pltpu.VMEM((4, 8, LANES), F32),
        pltpu.VMEM((LANES, LANES), F32),
        pltpu.VMEM((2 * PW, 2 * PW), BF16),
        pltpu.VMEM((2 * PW, 2 * PW), BF16),
        pltpu.VMEM((2 * PW, slots), BF16),
        pltpu.VMEM((2 * PW, 2 * PW), F32),
    ]
    scratch += [pltpu.VMEM((2 * PW, slots), BF16)] * number
    scratch += [pltpu.VMEM((2 * PW, slots), F32)] * number
    scratch += [pltpu.VMEM((2, 16, slots), F32)] * number
    scratch += [pltpu.VMEM((16, slots), I32)] * number
    if final:
        out_specs.append(pl.BlockSpec((None, 2 * PW + 16, PW), lambda s, i: (jnp.maximum(s - 1, 0), 0, 0)))
        out_shape.append(jax.ShapeDtypeStruct((steps, 2 * PW + 16, PW), BF16))
    zeros = 0
    if tile_columns:
        width = min(tile_columns, 4 * PW)
        zeros = tile_columns // width
        out_specs.append(pl.BlockSpec(memory_space=pltpu.HBM))
        out_shape.append(jax.ShapeDtypeStruct((2, patch_rows, tile_columns), F32))
        scratch += [pltpu.VMEM((2, patch_rows, width), F32), pltpu.SemaphoreType.DMA((zeros,))]
    return pl.pallas_call(
        functools.partial(
            residual_kernel, sources=number, capacity=capacity, first=first, final=final,
            resumed=before is not None, zeros=zeros, support=kernels.shape[1] // 4,
        ),
        grid_spec=pltpu.PrefetchScalarGridSpec(
            num_scalar_prefetch=1, grid=(steps + 1,), in_specs=in_specs, out_specs=out_specs, scratch_shapes=scratch
        ),
        out_shape=out_shape,
        compiler_params=pltpu.CompilerParams(vmem_limit_bytes=VMEM_LIMIT),
        cost_estimate=pl.CostEstimate(
            flops=steps * number * slots * 16 * PW * PW, bytes_accessed=steps * 65536, transcendentals=0
        ),
        name="degrid_and_grid",
    )(info, *operands)


def place_own_kernel(info_ref, place_ref, *refs, groups, capacity, per_slab):
    own_refs = refs[:groups]
    tile_ref, sem = refs[groups + 1 :]
    slab_start = place_ref[1] * per_slab
    total = info_ref[0, capacity]
    slots = [ref.at[k] for ref in own_refs for k in range(ref.shape[0])]

    def each(act):
        for k in range(capacity):
            local = info_ref[0, k] - slab_start

            @pl.when((k < total) & (local >= 0) & (local < per_slab))
            def _():
                cols = pl.ds(pl.multiple_of(local * PW, PW), PW)
                act(pltpu.make_async_copy(slots[k], tile_ref.at[:, :, cols], sem.at[k]))

    each(lambda copy: copy.start())
    each(lambda copy: copy.wait())


def place_received_kernel(info_ref, place_ref, received_ref, *refs, groups, capacity, per_slab, reread):
    own_refs = refs[:groups]
    tile_ref, sum_ref, sem = refs[groups + 1 :]
    slab_start = place_ref[1] * per_slab
    total = info_ref[0, capacity]
    slots = [ref.at[k] for ref in own_refs for k in range(ref.shape[0])]
    number = received_ref.shape[0]
    columns = [jnp.max(received_ref[k, 2 * PW :].astype(F32)).astype(I32) for k in range(number)]

    def each(act):
        for k in range(number):
            local = columns[k] - slab_start

            @pl.when((local >= 0) & (local < per_slab))
            def _():
                cols = pl.ds(pl.multiple_of(local * PW, PW), PW)
                act(k, pltpu.make_async_copy(sum_ref.at[k], tile_ref.at[:, :, cols], sem.at[k]))

    def send(k, copy):
        if reread:
            cols = pl.ds(pl.multiple_of((columns[k] - slab_start) * PW, PW), PW)
            there = pltpu.make_async_copy(tile_ref.at[:, :, cols], sum_ref.at[k], sem.at[k])
            there.start()
            there.wait()
            sum_ref[k, 0] += received_ref[k, 0:PW].astype(F32)
            sum_ref[k, 1] += received_ref[k, PW : 2 * PW].astype(F32)
            copy.start()
            return
        sum_ref[k, 0] = received_ref[k, 0:PW].astype(F32)
        sum_ref[k, 1] = received_ref[k, PW : 2 * PW].astype(F32)
        for j in range(capacity):

            @pl.when((j < total) & (info_ref[0, j] == columns[k]))
            def _():
                sum_ref[k] += slots[j][...]

        copy.start()

    each(send)
    each(lambda k, copy: copy.wait())


def place_patches(kernel, info, place, received, own, tile, per_slab, reread=False):
    groups = len(own)
    capacity = sum(patches.shape[0] for patches in own)
    scratch = [pltpu.SemaphoreType.DMA((capacity,))]
    if received:
        number, _, width = received[0].shape
        scratch = [pltpu.VMEM((number, 2, tile.shape[1], PW), F32), pltpu.SemaphoreType.DMA((number,))]
        kernel = functools.partial(kernel, reread=reread)
    operands = [*received, *own]
    return pl.pallas_call(
        functools.partial(kernel, groups=groups, capacity=capacity, per_slab=per_slab),
        grid_spec=pltpu.PrefetchScalarGridSpec(
            num_scalar_prefetch=2,
            grid=(1,),
            in_specs=[whole_block(a.shape) for a in operands] + [pl.BlockSpec(memory_space=pltpu.HBM)],
            out_specs=pl.BlockSpec(memory_space=pltpu.HBM),
            scratch_shapes=scratch,
        ),
        out_shape=jax.ShapeDtypeStruct(tile.shape, tile.dtype),
        input_output_aliases={2 + len(operands): 0},
        compiler_params=pltpu.CompilerParams(vmem_limit_bytes=VMEM_LIMIT),
        name="place_received" if received else "place_own",
    )(info, place, *operands, tile)


def swap(array, axis, distance):
    size = lax.axis_size(axis)
    return lax.ppermute(array, axis, [(i, i ^ distance) for i in range(size)])


def shards(model_grid, kernels, cover, cells, planes, observed, weights):
    tiles = lax.axis_size("grid")
    slabs = lax.axis_size("vis")
    per_tile = model_grid.shape[2] // PW
    per_slab = per_tile // slabs
    capacity = 2 * cover.shape[1] // tiles
    place = jnp.stack([lax.axis_index("grid"), lax.axis_index("vis")]).astype(I32)
    info, *pairs = pack(place, cover, cells, planes, observed, weights, tiles, per_tile, per_slab)
    arrived = [pairs[0]] + [swap(pairs[i], "grid", 2 * i) for i in range(1, tiles // 2)]
    run = functools.partial(residual, info, model_grid=model_grid, kernels=kernels, capacity=capacity)
    both = lambda pair: ((pair, 0), (swap(pair, "grid", 1), 1))
    before, tile = run(sources=both(arrived[0]), first=0, steps=capacity, tile_columns=per_slab * PW)
    before, *arrived[1:] = lax.optimization_barrier((before, *arrived[1:]))
    sources = [both(pair) for pair in arrived[1:]]
    while len(sources) > 3:
        (before,) = run(sources=sources.pop(0), first=0, steps=capacity, before=before)
    sources = sum(sources, ())
    own, received = [], []
    for first, end in ((0, 5 * capacity // 8), (5 * capacity // 8, capacity)):
        patches, send = run(sources=sources, first=first, steps=end - first, before=before, final=True)
        own.append(patches)
        received.append([swap(send, "vis", v) for v in range(1, slabs)])
    tile = place_patches(place_own_kernel, info, place, [], own, tile, per_slab)
    for group in received:
        for patches in group:
            tile = place_patches(place_received_kernel, info, place, [patches], own, tile, per_slab, slabs > 2)
    return tile


def solution(mesh):
    placed = (
        P("chan", "grid", None),
        P(),
        P(("chan", "vis"), None),
        P(("chan", "vis"), None, "grid"),
        P(("chan", "vis"), None, "grid"),
        P("chan", "vis", None, "grid"),
        P(("chan", "vis"), None, "grid"),
    )
    return jax.shard_map(
        shards, mesh=mesh, in_specs=placed, out_specs=P("chan", "grid", "vis"), check_vma=False
    )
```

```python
import functools

import jax
import jax.numpy as jnp
from jax import lax
from jax.experimental import pallas as pl
from jax.experimental.pallas import tpu as pltpu
from jax.sharding import PartitionSpec as P

PW = 128
LANES = 128
FIELDS = 5
PLANE_SHIFT = 12
BF16 = jnp.bfloat16
F32 = jnp.float32
I32 = jnp.int32
VMEM_LIMIT = 48 * 1024 * 1024
EMPTY = 255


def round_up(value, unit):
    return -(-value // unit) * unit


def whole_block(shape):
    return pl.BlockSpec(shape, lambda *_: (0,) * len(shape))


def iota(shape, dim):
    return lax.broadcasted_iota(I32, shape, dim)


def pack_kernel(
    place_ref, cover_hbm, cells_hbm, planes_hbm, observed_hbm, weights_hbm, info_ref, *refs,
    count, tiles, per_tile, per_slab, capacity, rows,
):
    outs = refs[: tiles // 2]
    cover_ref, cells_ref, planes_ref, observed_ref, weights_ref, sem = refs[tiles // 2 :]
    sources = (cover_hbm, cells_hbm, planes_hbm, observed_hbm, weights_hbm)
    targets = (cover_ref, cells_ref, planes_ref, observed_ref, weights_ref)
    copies = [pltpu.make_async_copy(x, y, sem.at[i]) for i, (x, y) in enumerate(zip(sources, targets))]
    for copy in copies:
        copy.start()
    me = place_ref[:, 0:1]
    slab = place_ref[:, 1:2]
    copies[0].wait()
    cover_row = cover_ref[...]
    across = jnp.broadcast_to(cover_row, (count, count))
    left = iota((count, count), 0)
    right = iota((count, count), 1)
    cover_col = jnp.sum(jnp.where(left == right, across, 0), axis=1, keepdims=True)

    def order_key(patch, entry):
        owner = patch // per_tile
        foreign = jnp.where((patch - owner * per_tile) // per_slab == slab, 1, 0)
        return owner, foreign * count + entry

    owner_i, key_i = order_key(cover_col, iota((count, 1), 0))
    owner_j, key_j = order_key(cover_row, iota((1, count), 1))
    same = owner_i == owner_j
    rank_row = jnp.sum(jnp.where(same & (key_i < key_j), 1, 0), axis=0, keepdims=True)
    rank_col = jnp.sum(jnp.where(same & (key_j < key_i), 1, 0), axis=1, keepdims=True)

    slot = iota((count, LANES), 1)
    own = (owner_i == me) & (rank_col == slot)
    column = cover_col - owner_i * per_tile
    listed = jnp.sum(jnp.where(own, column + 1, 0), axis=0, keepdims=True)
    total = jnp.sum(jnp.where(owner_i == me, 1, 0), axis=0, keepdims=True)
    lane = iota((1, LANES), 1)
    info = jnp.where(lane < capacity, listed - 1, jnp.where(lane == capacity, total, 0))
    info_ref[...] = jnp.broadcast_to(info, info_ref.shape)

    route = (owner_j ^ me) * capacity + rank_row
    spread = (iota((count, FIELDS * count), 1) % count == iota((count, FIELDS * count), 0)).astype(F32)
    wide = jnp.dot(
        jnp.broadcast_to(route.astype(F32), (8, count)).astype(BF16), spread.astype(BF16),
        preferred_element_type=F32,
    )[0:1].astype(I32)
    field_j = iota((1, FIELDS * count), 1) // count
    for copy in copies[1:]:
        copy.wait()
    cells = cells_ref[0]
    row_off = cells // PW
    plane = planes_ref[0]
    coded = (row_off + PW).astype(F32) * 2.0**-PLANE_SHIFT
    for bit in (1, 2, 4, 8, 16):
        coded = jnp.where((plane & bit) != 0, coded * 2.0**bit, coded)
    fields = [coded, cells - row_off * PW, observed_ref[0, 0], observed_ref[1, 0], weights_ref[0]]
    data = jnp.concatenate([field.astype(F32).astype(BF16) for field in fields], axis=0)
    line = iota((rows, FIELDS * count), 0)
    block = rows // FIELDS
    field_i = line // block
    half = (line - field_i * block) // capacity
    slot_i = (line - field_i * block) - half * capacity
    for m in range(0, tiles, 2):
        pick = (field_i == field_j) & (half < 2) & (wide == (m + half) * capacity + slot_i)
        rows_out = jnp.dot(pick.astype(F32).astype(BF16), data, preferred_element_type=F32)
        outs[m // 2][...] = rows_out.astype(BF16)


def in_hbm(array):
    return pltpu.with_memory_space_constraint(array, pltpu.HBM)


def pack(place, cover, cells, planes, observed, weights, tiles, per_tile, per_slab):
    count, slots = cells.shape[1:]
    capacity = 2 * count // tiles
    rows = FIELDS * round_up(2 * capacity, 16)
    arrays = (cover, cells, planes, observed, weights)
    outputs = [((8, LANES), I32)] + [((rows, slots), BF16)] * (tiles // 2)
    return pl.pallas_call(
        functools.partial(
            pack_kernel, count=count, tiles=tiles, per_tile=per_tile, per_slab=per_slab,
            capacity=capacity, rows=rows,
        ),
        in_specs=[pl.BlockSpec(memory_space=pltpu.VMEM)] + [pl.BlockSpec(memory_space=pltpu.HBM)] * len(arrays),
        out_specs=[pl.BlockSpec(memory_space=pltpu.VMEM)] * len(outputs),
        scratch_shapes=[pltpu.VMEM(a.shape, a.dtype) for a in arrays] + [pltpu.SemaphoreType.DMA((len(arrays),))],
        out_shape=[jax.ShapeDtypeStruct(shape, dtype) for shape, dtype in outputs],
        compiler_params=pltpu.CompilerParams(vmem_limit_bytes=VMEM_LIMIT),
        name="pack_by_tile",
    )(place, *[in_hbm(a) for a in arrays])


def fill_tables(kern_ref, wide_ref, table_ref, support):
    wide_ref[...] = jnp.zeros_like(wide_ref)
    wide_ref[0 : kern_ref.shape[0], 0 : kern_ref.shape[1]] = kern_ref[...]
    flipped = wide_ref[...].T
    zero = jnp.zeros((8 - support, LANES), F32)
    for group in range(4):
        taps = [flipped[support * group + i : support * group + i + 1] for i in reversed(range(support))]
        table_ref[group] = jnp.concatenate([zero, *taps], axis=0)


def pick(array, index, axis):
    return lax.gather(
        array,
        index[..., None],
        lax.GatherDimensionNumbers(
            offset_dims=(), collapsed_slice_dims=(axis,), start_index_map=(axis,),
            operand_batching_dims=(1 - axis,), start_indices_batching_dims=(1 - axis,),
        ),
        slice_sizes=(1, 1),
        mode=lax.GatherScatterMode.PROMISE_IN_BOUNDS,
    )


def tap_places(offset):
    place = jnp.broadcast_to(offset, (16, LANES)) + (15 - iota((16, LANES), 0))
    return place & 7, place >> 3


def wrapped(taps, places):
    return jnp.concatenate([pick(taps, places[0:8], 0), pick(taps, places[8:16], 0)], axis=0)


def expand(ref, base, cols, rows, group):
    for q in range(PW // 16):
        ref[base + 16 * q : base + 16 * q + 16, cols] = jnp.where(group == BF16(2 * q + 1), rows, BF16(0))


def unpack(block_ref, half, capacity, f_ref, i_ref, base):
    block = block_ref.shape[0] // FIELDS
    coded = block_ref[0:block].astype(F32)[half * capacity : (half + 1) * capacity] * 2.0**PLANE_SHIFT
    plane = jnp.zeros_like(coded)
    for bit in (16, 8, 4, 2, 1):
        hit = coded >= PW * 2.0**bit
        coded = jnp.where(hit, coded * 2.0**-bit, coded)
        plane = jnp.where(hit, plane + bit, plane)
    decoded = jnp.concatenate([coded - PW, plane], axis=0)
    decoded = jnp.concatenate([decoded] + [jnp.zeros_like(coded)] * (block // capacity * 2 - 2), axis=0)
    data = jnp.concatenate([decoded.astype(BF16), block_ref[block:]], axis=0)
    shape = (8 * capacity, data.shape[0])
    line = iota(shape, 0)
    field = line & 7
    slot = line >> 3
    start = jnp.where(field == 0, 0, jnp.where(field == 2, capacity, -1))
    first = decoded.shape[0] - block
    later = first + (field - jnp.where(field > 2, 1, 0)) * block + half * capacity
    order = iota(shape, 1) == jnp.where(start >= 0, start, later) + slot
    order = order & (field < FIELDS + 1)
    fields = jnp.dot(order.astype(F32).astype(BF16), data, preferred_element_type=F32)
    whole = fields.astype(I32)
    for slot in range(capacity):
        f_ref[base + slot] = fields[8 * slot : 8 * slot + 8]
        i_ref[base + slot] = whole[8 * slot : 8 * slot + 8]


def degrid_start(i_ref, item, table_ref, wt_ref, u_ref, m_ref, v_ref, g_ref):
    for t in range(u_ref.shape[1] // LANES):
        cols = pl.ds(t * LANES, LANES)
        plane = jnp.broadcast_to(i_ref[item, 2:3, cols], (8, LANES))
        u_place, u_group = tap_places(i_ref[item, 0:1, cols])
        v_place, v_group = tap_places(i_ref[item, 1:2, cols])
        u_re = wrapped(pick(table_ref[0], plane, 1), u_place).astype(BF16)
        u_im = wrapped(pick(table_ref[1], plane, 1), u_place).astype(BF16)
        v_ref[0, :, cols] = wrapped(pick(table_ref[2], plane, 1), v_place)
        v_ref[1, :, cols] = wrapped(pick(table_ref[3], plane, 1), v_place)
        g_ref[:, cols] = v_group
        u_group = u_group.astype(F32).astype(BF16)
        expand(u_ref, 0, cols, u_re, u_group)
        expand(u_ref, PW, cols, u_im, u_group)
    m_ref[...] = jnp.dot(wt_ref[...], u_ref[...], preferred_element_type=F32)


def degrid_end(f_ref, item, u_ref, m_ref, s_ref, v_ref, g_ref, q_ref):
    for t in range(u_ref.shape[1] // LANES):
        cols = pl.ds(t * LANES, LANES)
        group = g_ref[:, cols]
        m_re = jnp.zeros((16, LANES), F32)
        m_im = jnp.zeros((16, LANES), F32)
        for q in range(PW // 16):
            hit = group == 2 * q + 1
            m_re = jnp.where(hit, m_ref[16 * q : 16 * q + 16, cols], m_re)
            m_im = jnp.where(hit, m_ref[PW + 16 * q : PW + 16 * q + 16, cols], m_im)
        v_re = v_ref[0, :, cols]
        v_im = v_ref[1, :, cols]
        model_re = jnp.sum(m_re * v_re - m_im * v_im, axis=0, keepdims=True)
        model_im = jnp.sum(m_re * v_im + m_im * v_re, axis=0, keepdims=True)
        weight = f_ref[item, 5:6, cols]
        res_re = weight * (f_ref[item, 3:4, cols] - model_re)
        res_im = weight * (f_ref[item, 4:5, cols] - model_im)
        s_re = (res_re * v_re + res_im * v_im).astype(BF16)
        s_im = (res_im * v_re - res_re * v_im).astype(BF16)
        group = group.astype(F32).astype(BF16)
        expand(s_ref, 0, cols, s_re, group)
        expand(s_ref, PW, cols, s_im, group)
    q_ref[...] += lax.dot_general(
        u_ref[...], s_ref[...], (((1,), (1,)), ((), ())), preferred_element_type=F32
    )


def residual_kernel(info_ref, *refs, halves, capacity, first, final, begin, zeros, support, unpacked, keep, per):
    refs = list(refs)
    take = lambda number: [refs.pop(0) for _ in range(number)]
    sources = len(halves)
    block_refs = [] if unpacked else take(sources)
    f_ref, i_ref = take(2) if unpacked else (None, None)
    if begin:
        model_refs = take(per)
        (kern_ref,) = take(1)
        patch_ref, tile_ref, wt_ref, table_ref = take(4)
    else:
        wt_ref, table_ref, before_ref = take(3)
        (patch_ref,) = take(1)
    send_ref = take(1)[0] if final else None
    if not unpacked:
        f_ref, i_ref = take(2)
    s_ref, q_ref = take(2)
    u, m, v, g = (take(sources) for _ in range(4))
    step = pl.program_id(0)
    k = first + (step - 1) * per
    if begin:
        wide_ref, zero_ref, sem = take(3)
        total = info_ref[0, capacity]
        width = zero_ref.shape[2]
        clears = [
            pltpu.make_async_copy(zero_ref, tile_ref.at[:, :, pl.ds(i * width, width)], sem.at[i])
            for i in range(zeros)
        ]
    else:
        lane = iota((1, LANES), 1)
        listed = info_ref[0:1]
        total = jnp.sum(jnp.where(lane == capacity, listed, 0))

    def turn():
        for i in range(per if begin else 0):
            slot = jnp.minimum(first + step * per + i, capacity - 1)
            real = model_refs[i][0].T
            imag = model_refs[i][1].T
            wt_ref[slot, 0:PW, 0:PW] = real
            wt_ref[slot, 0:PW, PW:] = -imag
            wt_ref[slot, PW:, 0:PW] = imag
            wt_ref[slot, PW:, PW:] = real

    def start(slot, b):
        degrid_start(i_ref, b * capacity + slot, table_ref, wt_ref.at[slot], u[b], m[b], v[b], g[b])

    def end(slot, b, i):
        degrid_end(f_ref, b * capacity + slot, u[b], m[b], s_ref, v[b], g[b], q_ref.at[i])

    @pl.when(step == 0)
    def _():
        if begin:
            zero_ref[...] = jnp.zeros_like(zero_ref)
            for copy in clears:
                copy.start()
            fill_tables(kern_ref, wide_ref, table_ref, support)
        for b, block_ref in enumerate(block_refs):
            unpack(block_ref, halves[b], capacity, f_ref, i_ref, b * capacity)
        turn()
        start(first, 0)

    @pl.when((step > 0) & (k < total))
    def _():
        turn()
        for i in range(per):
            q_ref[i] = jnp.zeros_like(q_ref[i])
            for b in range(sources):
                end(k + i, b, i)
                if b + 1 < sources:
                    start(k + i, b + 1)
                else:
                    start(jnp.minimum(k + i + 1, capacity - 1), 0)
            out = (step - 1) * per + i
            q_re = q_ref[i, 0:PW, 0:PW] + q_ref[i, PW:, PW:]
            q_im = q_ref[i, 0:PW, PW:] - q_ref[i, PW:, 0:PW]
            if not begin:
                q_re += before_ref[k + i, 0]
                q_im += before_ref[k + i, 1]
            patch_ref[out, 0] = q_re
            patch_ref[out, 1] = q_im
            if final:
                send_ref[out, 0:PW] = q_re.astype(BF16)
                send_ref[out, PW : 2 * PW] = q_im.astype(BF16)

    if final:
        for i in range(per):
            column = jnp.sum(jnp.where(lane == k + i, listed, 0), axis=1, keepdims=True)
            column = jnp.where(k + i < total, column, EMPTY).astype(F32).astype(BF16)
            send_ref[jnp.maximum((step - 1) * per + i, 0), 2 * PW :] = jnp.broadcast_to(column, (16, PW))
    if begin:

        @pl.when(step == pl.num_programs(0) - 1)
        def _():
            for copy in clears:
                copy.wait()


def residual(
    info, sources, capacity, first, steps, model_grid=None, kernels=None, tile_columns=0,
    prepared=None, before=None, final=False, unpacked=None, keep=False, per=1,
):
    begin = prepared is None
    slots = sources[0][0].shape[1]
    number = len(sources)
    in_vmem = pl.BlockSpec(memory_space=pltpu.VMEM)
    operands = [array for array, _ in sources] if unpacked is None else list(unpacked)
    in_specs = [in_vmem for _ in operands]
    out_specs = [in_vmem]
    out_shape = [jax.ShapeDtypeStruct((steps, 2, PW, PW), F32)]
    support, zeros, more = 0, 0, []
    if begin:
        support = kernels.shape[1] // 4
        width = min(tile_columns, 4 * PW)
        zeros = tile_columns // width
        patch_of = lambda s, i, j: (0, 0, jnp.maximum(i[0, jnp.minimum(s * per + j, capacity - 1)], 0))
        in_specs += [pl.BlockSpec((2, PW, PW), functools.partial(patch_of, j=j)) for j in range(per)]
        in_specs.append(whole_block(kernels.shape))
        operands += [in_hbm(model_grid)] * per + [in_hbm(kernels)]
        out_specs += [pl.BlockSpec(memory_space=pltpu.HBM), in_vmem, in_vmem]
        out_shape += [
            jax.ShapeDtypeStruct((2, PW, tile_columns), F32),
            jax.ShapeDtypeStruct((capacity, 2 * PW, 2 * PW), BF16),
            jax.ShapeDtypeStruct((4, 8, LANES), F32),
        ]
        more = [
            pltpu.VMEM((LANES, LANES), F32),
            pltpu.VMEM((2, PW, width), F32),
            pltpu.SemaphoreType.DMA((zeros,)),
        ]
    else:
        in_specs = [in_vmem] + in_specs + [in_vmem] * 3
        operands += [*prepared, before]
    if final:
        out_specs.append(in_vmem)
        out_shape.append(jax.ShapeDtypeStruct((steps, 2 * PW + 16, PW), BF16))
    fields = [((number * capacity, 8, slots), dtype) for dtype in (F32, I32)]
    scratch = [pltpu.VMEM((2 * PW, slots), BF16), pltpu.VMEM((per, 2 * PW, 2 * PW), F32)]
    if keep:
        out_specs += [in_vmem] * 2
        out_shape += [jax.ShapeDtypeStruct(*field) for field in fields]
    elif unpacked is None:
        scratch = [pltpu.VMEM(*field) for field in fields] + scratch
    scratch += [pltpu.VMEM((2 * PW, slots), BF16)] * number
    scratch += [pltpu.VMEM((2 * PW, slots), F32)] * number
    scratch += [pltpu.VMEM((2, 16, slots), F32)] * number
    scratch += [pltpu.VMEM((16, slots), I32)] * number
    return pl.pallas_call(
        functools.partial(
            residual_kernel, halves=tuple(half for _, half in sources), capacity=capacity, first=first,
            final=final, begin=begin, zeros=zeros, support=support, unpacked=unpacked is not None, keep=keep,
            per=per,
        ),
        grid_spec=pltpu.PrefetchScalarGridSpec(
            num_scalar_prefetch=1 if begin else 0, grid=(steps // per + 1,), in_specs=in_specs, out_specs=out_specs,
            scratch_shapes=scratch + more,
        ),
        out_shape=out_shape,
        compiler_params=pltpu.CompilerParams(vmem_limit_bytes=VMEM_LIMIT),
        cost_estimate=pl.CostEstimate(
            flops=steps * number * slots * 16 * PW * PW, bytes_accessed=steps * 65536, transcendentals=0
        ),
        name="degrid_and_grid",
    )(info, *operands)


def place_own_kernel(info_ref, place_ref, *refs, groups, capacity, per_slab):
    own_refs = refs[:groups]
    tile_ref, sem = refs[groups + 1 :]
    slab_start = place_ref[1] * per_slab
    total = info_ref[0, capacity]
    slots = [ref.at[k] for ref in own_refs for k in range(ref.shape[0])]

    def each(act):
        for k in range(capacity):
            local = info_ref[0, k] - slab_start

            @pl.when((k < total) & (local >= 0) & (local < per_slab))
            def _():
                cols = pl.ds(pl.multiple_of(local * PW, PW), PW)
                act(pltpu.make_async_copy(slots[k], tile_ref.at[:, :, cols], sem.at[k]))

    each(lambda copy: copy.start())
    each(lambda copy: copy.wait())


def place_received_kernel(info_ref, place_ref, received_ref, *refs, groups, capacity, per_slab, reread):
    own_refs = refs[:groups]
    tile_ref, sum_ref, sem = refs[groups + 1 :]
    slab_start = place_ref[1] * per_slab
    total = info_ref[0, capacity]
    slots = [ref.at[k] for ref in own_refs for k in range(ref.shape[0])]
    number = received_ref.shape[0]
    columns = [jnp.max(received_ref[k, 2 * PW :].astype(F32)).astype(I32) for k in range(number)]

    def each(act):
        for k in range(number):
            local = columns[k] - slab_start

            @pl.when((local >= 0) & (local < per_slab))
            def _():
                cols = pl.ds(pl.multiple_of(local * PW, PW), PW)
                act(k, pltpu.make_async_copy(sum_ref.at[k], tile_ref.at[:, :, cols], sem.at[k]))

    def send(k, copy):
        if reread:
            cols = pl.ds(pl.multiple_of((columns[k] - slab_start) * PW, PW), PW)
            there = pltpu.make_async_copy(tile_ref.at[:, :, cols], sum_ref.at[k], sem.at[k])
            there.start()
            there.wait()
            sum_ref[k, 0] += received_ref[k, 0:PW].astype(F32)
            sum_ref[k, 1] += received_ref[k, PW : 2 * PW].astype(F32)
            copy.start()
            return
        sum_ref[k, 0] = received_ref[k, 0:PW].astype(F32)
        sum_ref[k, 1] = received_ref[k, PW : 2 * PW].astype(F32)
        for j in range(capacity):

            @pl.when((j < total) & (info_ref[0, j] == columns[k]))
            def _():
                sum_ref[k] += slots[j][...]

        copy.start()

    each(send)
    each(lambda k, copy: copy.wait())


def place_patches(kernel, info, place, received, own, tile, per_slab, reread=False):
    groups = len(own)
    capacity = sum(patches.shape[0] for patches in own)
    scratch = [pltpu.SemaphoreType.DMA((capacity,))]
    if received:
        number, _, width = received[0].shape
        scratch = [pltpu.VMEM((number, 2, tile.shape[1], PW), F32), pltpu.SemaphoreType.DMA((number,))]
        kernel = functools.partial(kernel, reread=reread)
    operands = [*received, *own]
    return pl.pallas_call(
        functools.partial(kernel, groups=groups, capacity=capacity, per_slab=per_slab),
        grid_spec=pltpu.PrefetchScalarGridSpec(
            num_scalar_prefetch=2,
            grid=(1,),
            in_specs=[pl.BlockSpec(memory_space=pltpu.VMEM)] * len(operands)
            + [pl.BlockSpec(memory_space=pltpu.HBM)],
            out_specs=pl.BlockSpec(memory_space=pltpu.HBM),
            scratch_shapes=scratch,
        ),
        out_shape=jax.ShapeDtypeStruct(tile.shape, tile.dtype),
        input_output_aliases={2 + len(operands): 0},
        compiler_params=pltpu.CompilerParams(vmem_limit_bytes=VMEM_LIMIT),
        name="place_received" if received else "place_own",
    )(info, place, *operands, tile)


def swap(array, axis, distance):
    size = lax.axis_size(axis)
    return lax.ppermute(array, axis, [(i, i ^ distance) for i in range(size)])


def shards(model_grid, kernels, cover, cells, planes, observed, weights):
    tiles = lax.axis_size("grid")
    slabs = lax.axis_size("vis")
    per_tile = model_grid.shape[2] // PW
    per_slab = per_tile // slabs
    capacity = 2 * cover.shape[1] // tiles
    place = jnp.stack([lax.axis_index("grid"), lax.axis_index("vis")]).astype(I32)
    lane = lax.broadcasted_iota(I32, (1, LANES), 1)
    places = jnp.where(lane == 0, place[0], place[1])
    info, *pairs = pack(places, cover, cells, planes, observed, weights, tiles, per_tile, per_slab)
    arrived = [swap(pairs[i], "grid", 2 * i) for i in reversed(range(1, tiles // 2))]
    arrived = [pairs[0]] + arrived[::-1]
    both = lambda pair: ((pair, 0), (swap(pair, "grid", 1), 1))
    near = both(arrived[1])
    early = both(arrived[0]) + near[:1]
    before, tile, *prepared = residual(
        info, early, capacity, 0, capacity, model_grid=model_grid, kernels=kernels,
        tile_columns=per_slab * PW, per=2,
    )
    run = functools.partial(residual, info, capacity=capacity, prepared=prepared)
    before, *rest = lax.optimization_barrier((before, *arrived[2:]))
    sources = near[1:] + sum((both(pair) for pair in rest), ())
    while len(sources) > 6:
        (before,) = run(sources[:4], first=0, steps=capacity, before=before)
        sources = sources[4:]
    own, received = [], []
    unpacked = None
    for first, end in ((0, 5 * capacity // 8), (5 * capacity // 8, capacity)):
        patches, send, *fields = run(
            sources, first=first, steps=end - first, before=before, final=True, unpacked=unpacked,
            keep=unpacked is None,
        )
        unpacked = unpacked or fields
        own.append(patches)
        received.append([swap(send, "vis", v) for v in range(1, slabs)])
    tile = place_patches(place_own_kernel, info, place, [], own, tile, per_slab)
    for group in received:
        for patches in group:
            tile = place_patches(place_received_kernel, info, place, [patches], own, tile, per_slab, slabs > 2)
    return tile


def solution(mesh):
    placed = (
        P("chan", "grid", None),
        P(),
        P(("chan", "vis"), None),
        P(("chan", "vis"), None, "grid"),
        P(("chan", "vis"), None, "grid"),
        P("chan", "vis", None, "grid"),
        P(("chan", "vis"), None, "grid"),
    )
    return jax.shard_map(
        shards, mesh=mesh, in_specs=placed, out_specs=P("chan", "grid", "vis"), check_vma=False
    )
```

```python
import functools

import jax
import jax.numpy as jnp
from jax import lax
from jax.experimental import pallas as pl
from jax.experimental.pallas import tpu as pltpu
from jax.sharding import PartitionSpec as P

PW = 128
LANES = 128
FIELDS = 5
PLANE_SHIFT = 12
BF16 = jnp.bfloat16
F32 = jnp.float32
I32 = jnp.int32
VMEM_LIMIT = 48 * 1024 * 1024
EMPTY = 255


def round_up(value, unit):
    return -(-value // unit) * unit


def whole_block(shape):
    return pl.BlockSpec(shape, lambda *_: (0,) * len(shape))


def iota(shape, dim):
    return lax.broadcasted_iota(I32, shape, dim)


def pack_kernel(
    place_ref, cover_hbm, cells_hbm, planes_hbm, observed_hbm, weights_hbm, info_ref, *refs,
    count, tiles, per_tile, per_slab, capacity, rows,
):
    outs = refs[: tiles // 2]
    cover_ref, cells_ref, planes_ref, observed_ref, weights_ref, sem = refs[tiles // 2 :]
    sources = (cover_hbm, cells_hbm, planes_hbm, observed_hbm, weights_hbm)
    targets = (cover_ref, cells_ref, planes_ref, observed_ref, weights_ref)
    copies = [pltpu.make_async_copy(x, y, sem.at[i]) for i, (x, y) in enumerate(zip(sources, targets))]
    for copy in copies:
        copy.start()
    me = place_ref[:, 0:1]
    slab = place_ref[:, 1:2]
    copies[0].wait()
    cover_row = cover_ref[...]
    across = jnp.broadcast_to(cover_row, (count, count))
    left = iota((count, count), 0)
    right = iota((count, count), 1)
    cover_col = jnp.sum(jnp.where(left == right, across, 0), axis=1, keepdims=True)

    def order_key(patch, entry):
        owner = patch // per_tile
        foreign = jnp.where((patch - owner * per_tile) // per_slab == slab, 1, 0)
        return owner, foreign * count + entry

    owner_i, key_i = order_key(cover_col, iota((count, 1), 0))
    owner_j, key_j = order_key(cover_row, iota((1, count), 1))
    same = owner_i == owner_j
    rank_row = jnp.sum(jnp.where(same & (key_i < key_j), 1, 0), axis=0, keepdims=True)
    rank_col = jnp.sum(jnp.where(same & (key_j < key_i), 1, 0), axis=1, keepdims=True)

    slot = iota((count, LANES), 1)
    own = (owner_i == me) & (rank_col == slot)
    column = cover_col - owner_i * per_tile
    listed = jnp.sum(jnp.where(own, column + 1, 0), axis=0, keepdims=True)
    total = jnp.sum(jnp.where(owner_i == me, 1, 0), axis=0, keepdims=True)
    lane = iota((1, LANES), 1)
    info = jnp.where(lane < capacity, listed - 1, jnp.where(lane == capacity, total, 0))
    info_ref[...] = jnp.broadcast_to(info, info_ref.shape)

    route = (owner_j ^ me) * capacity + rank_row
    spread = (iota((count, FIELDS * count), 1) % count == iota((count, FIELDS * count), 0)).astype(F32)
    wide = jnp.dot(
        jnp.broadcast_to(route.astype(F32), (8, count)).astype(BF16), spread.astype(BF16),
        preferred_element_type=F32,
    )[0:1].astype(I32)
    field_j = iota((1, FIELDS * count), 1) // count
    for copy in copies[1:]:
        copy.wait()
    cells = cells_ref[0]
    row_off = cells // PW
    plane = planes_ref[0]
    coded = (row_off + PW).astype(F32) * 2.0**-PLANE_SHIFT
    for bit in (1, 2, 4, 8, 16):
        coded = jnp.where((plane & bit) != 0, coded * 2.0**bit, coded)
    fields = [coded, cells - row_off * PW, observed_ref[0, 0], observed_ref[1, 0], weights_ref[0]]
    data = jnp.concatenate([field.astype(F32).astype(BF16) for field in fields], axis=0)
    line = iota((rows, FIELDS * count), 0)
    block = rows // FIELDS
    field_i = line // block
    half = (line - field_i * block) // capacity
    slot_i = (line - field_i * block) - half * capacity
    for m in range(0, tiles, 2):
        pick = (field_i == field_j) & (half < 2) & (wide == (m + half) * capacity + slot_i)
        rows_out = jnp.dot(pick.astype(F32).astype(BF16), data, preferred_element_type=F32)
        outs[m // 2][...] = rows_out.astype(BF16)


def in_hbm(array):
    return pltpu.with_memory_space_constraint(array, pltpu.HBM)


def pack(place, cover, cells, planes, observed, weights, tiles, per_tile, per_slab):
    count, slots = cells.shape[1:]
    capacity = 2 * count // tiles
    rows = FIELDS * round_up(2 * capacity, 16)
    arrays = (cover, cells, planes, observed, weights)
    outputs = [((8, LANES), I32)] + [((rows, slots), BF16)] * (tiles // 2)
    return pl.pallas_call(
        functools.partial(
            pack_kernel, count=count, tiles=tiles, per_tile=per_tile, per_slab=per_slab,
            capacity=capacity, rows=rows,
        ),
        in_specs=[pl.BlockSpec(memory_space=pltpu.VMEM)] + [pl.BlockSpec(memory_space=pltpu.HBM)] * len(arrays),
        out_specs=[pl.BlockSpec(memory_space=pltpu.VMEM)] * len(outputs),
        scratch_shapes=[pltpu.VMEM(a.shape, a.dtype) for a in arrays] + [pltpu.SemaphoreType.DMA((len(arrays),))],
        out_shape=[jax.ShapeDtypeStruct(shape, dtype) for shape, dtype in outputs],
        compiler_params=pltpu.CompilerParams(vmem_limit_bytes=VMEM_LIMIT),
        name="pack_by_tile",
    )(place, *[in_hbm(a) for a in arrays])


def fill_tables(kern_ref, wide_ref, table_ref, support):
    wide_ref[...] = jnp.zeros_like(wide_ref)
    wide_ref[0 : kern_ref.shape[0], 0 : kern_ref.shape[1]] = kern_ref[...]
    flipped = wide_ref[...].T
    zero = jnp.zeros((8 - support, LANES), F32)
    for group in range(4):
        taps = [flipped[support * group + i : support * group + i + 1] for i in reversed(range(support))]
        table_ref[group] = jnp.concatenate([zero, *taps], axis=0)


def pick(array, index, axis):
    return lax.gather(
        array,
        index[..., None],
        lax.GatherDimensionNumbers(
            offset_dims=(), collapsed_slice_dims=(axis,), start_index_map=(axis,),
            operand_batching_dims=(1 - axis,), start_indices_batching_dims=(1 - axis,),
        ),
        slice_sizes=(1, 1),
        mode=lax.GatherScatterMode.PROMISE_IN_BOUNDS,
    )


def tap_places(offset):
    place = jnp.broadcast_to(offset, (16, LANES)) + (15 - iota((16, LANES), 0))
    return place & 7, place >> 3


def wrapped(taps, places):
    return jnp.concatenate([pick(taps, places[0:8], 0), pick(taps, places[8:16], 0)], axis=0)


def expand(ref, base, cols, rows, group):
    for q in range(PW // 16):
        ref[base + 16 * q : base + 16 * q + 16, cols] = jnp.where(group == BF16(2 * q + 1), rows, BF16(0))


def unpack(block_ref, half, capacity, f_ref, i_ref, base):
    block = block_ref.shape[0] // FIELDS
    coded = block_ref[0:block].astype(F32)[half * capacity : (half + 1) * capacity] * 2.0**PLANE_SHIFT
    plane = jnp.zeros_like(coded)
    for bit in (16, 8, 4, 2, 1):
        hit = coded >= PW * 2.0**bit
        coded = jnp.where(hit, coded * 2.0**-bit, coded)
        plane = jnp.where(hit, plane + bit, plane)
    decoded = jnp.concatenate([coded - PW, plane], axis=0)
    decoded = jnp.concatenate([decoded] + [jnp.zeros_like(coded)] * (block // capacity * 2 - 2), axis=0)
    data = jnp.concatenate([decoded.astype(BF16), block_ref[block:]], axis=0)
    shape = (8 * capacity, data.shape[0])
    line = iota(shape, 0)
    field = line & 7
    slot = line >> 3
    start = jnp.where(field == 0, 0, jnp.where(field == 2, capacity, -1))
    first = decoded.shape[0] - block
    later = first + (field - jnp.where(field > 2, 1, 0)) * block + half * capacity
    order = iota(shape, 1) == jnp.where(start >= 0, start, later) + slot
    order = order & (field < FIELDS + 1)
    fields = jnp.dot(order.astype(F32).astype(BF16), data, preferred_element_type=F32)
    whole = fields.astype(I32)
    for slot in range(capacity):
        f_ref[base + slot] = fields[8 * slot : 8 * slot + 8]
        i_ref[base + slot] = whole[8 * slot : 8 * slot + 8]


def degrid_start(i_ref, item, table_ref, wt_ref, u_ref, m_ref, v_ref, g_ref):
    for t in range(u_ref.shape[1] // LANES):
        cols = pl.ds(t * LANES, LANES)
        plane = jnp.broadcast_to(i_ref[item, 2:3, cols], (8, LANES))
        u_place, u_group = tap_places(i_ref[item, 0:1, cols])
        v_place, v_group = tap_places(i_ref[item, 1:2, cols])
        u_re = wrapped(pick(table_ref[0], plane, 1), u_place).astype(BF16)
        u_im = wrapped(pick(table_ref[1], plane, 1), u_place).astype(BF16)
        v_ref[0, :, cols] = wrapped(pick(table_ref[2], plane, 1), v_place)
        v_ref[1, :, cols] = wrapped(pick(table_ref[3], plane, 1), v_place)
        g_ref[:, cols] = v_group
        u_group = u_group.astype(F32).astype(BF16)
        expand(u_ref, 0, cols, u_re, u_group)
        expand(u_ref, PW, cols, u_im, u_group)
    m_ref[...] = jnp.dot(wt_ref[...], u_ref[...], preferred_element_type=F32)


def degrid_end(f_ref, item, u_ref, m_ref, s_ref, v_ref, g_ref, q_ref):
    for t in range(u_ref.shape[1] // LANES):
        cols = pl.ds(t * LANES, LANES)
        group = g_ref[:, cols]
        m_re = jnp.zeros((16, LANES), F32)
        m_im = jnp.zeros((16, LANES), F32)
        for q in range(PW // 16):
            hit = group == 2 * q + 1
            m_re = jnp.where(hit, m_ref[16 * q : 16 * q + 16, cols], m_re)
            m_im = jnp.where(hit, m_ref[PW + 16 * q : PW + 16 * q + 16, cols], m_im)
        v_re = v_ref[0, :, cols]
        v_im = v_ref[1, :, cols]
        model_re = jnp.sum(m_re * v_re - m_im * v_im, axis=0, keepdims=True)
        model_im = jnp.sum(m_re * v_im + m_im * v_re, axis=0, keepdims=True)
        weight = f_ref[item, 5:6, cols]
        res_re = weight * (f_ref[item, 3:4, cols] - model_re)
        res_im = weight * (f_ref[item, 4:5, cols] - model_im)
        s_re = (res_re * v_re + res_im * v_im).astype(BF16)
        s_im = (res_im * v_re - res_re * v_im).astype(BF16)
        group = group.astype(F32).astype(BF16)
        expand(s_ref, 0, cols, s_re, group)
        expand(s_ref, PW, cols, s_im, group)
    q_ref[...] += lax.dot_general(
        u_ref[...], s_ref[...], (((1,), (1,)), ((), ())), preferred_element_type=F32
    )


def residual_kernel(info_ref, *refs, halves, capacity, first, final, begin, zeros, support, unpacked, keep, per):
    refs = list(refs)
    take = lambda number: [refs.pop(0) for _ in range(number)]
    sources = len(halves)
    block_refs = [] if unpacked else take(sources)
    f_ref, i_ref = take(2) if unpacked else (None, None)
    if begin:
        model_refs = take(per)
        (kern_ref,) = take(1)
        patch_ref, tile_ref, wt_ref, table_ref = take(4)
    else:
        wt_ref, table_ref, before_ref = take(3)
        (patch_ref,) = take(1)
    send_ref = take(1)[0] if final else None
    if not unpacked:
        f_ref, i_ref = take(2)
    s_ref, q_ref = take(2)
    u, m, v, g = (take(sources) for _ in range(4))
    step = pl.program_id(0) if begin else 1
    k = first + (step - 1) * per
    if begin:
        wide_ref, zero_ref, sem = take(3)
        total = info_ref[0, capacity]
        width = zero_ref.shape[2]
        clears = [
            pltpu.make_async_copy(zero_ref, tile_ref.at[:, :, pl.ds(i * width, width)], sem.at[i])
            for i in range(zeros)
        ]
    else:
        lane = iota((1, LANES), 1)
        listed = info_ref[0:1]
        total = jnp.sum(jnp.where(lane == capacity, listed, 0))

    def turn():
        for i in range(per if begin else 0):
            slot = jnp.minimum(first + step * per + i, capacity - 1)
            real = model_refs[i][0].T
            imag = model_refs[i][1].T
            wt_ref[slot, 0:PW, 0:PW] = real
            wt_ref[slot, 0:PW, PW:] = -imag
            wt_ref[slot, PW:, 0:PW] = imag
            wt_ref[slot, PW:, PW:] = real

    def start(slot, b):
        degrid_start(i_ref, b * capacity + slot, table_ref, wt_ref.at[slot], u[b], m[b], v[b], g[b])

    def end(slot, b, i):
        degrid_end(f_ref, b * capacity + slot, u[b], m[b], s_ref, v[b], g[b], q_ref.at[i])

    def prepare():
        if begin:
            zero_ref[...] = jnp.zeros_like(zero_ref)
            for copy in clears:
                copy.start()
            fill_tables(kern_ref, wide_ref, table_ref, support)
        for b, block_ref in enumerate(block_refs):
            unpack(block_ref, halves[b], capacity, f_ref, i_ref, b * capacity)
        turn()
        start(first, 0)

    if begin:
        pl.when(step == 0)(prepare)

    @pl.when((step > 0) & (k < total))
    def _():
        turn()
        if not begin:
            prepare()
        for i in range(per):
            q_ref[i] = jnp.zeros_like(q_ref[i])
            for b in range(sources):
                end(k + i, b, i)
                if b + 1 < sources:
                    start(k + i, b + 1)
                else:
                    start(jnp.minimum(k + i + 1, capacity - 1), 0)
            out = (step - 1) * per + i
            q_re = q_ref[i, 0:PW, 0:PW] + q_ref[i, PW:, PW:]
            q_im = q_ref[i, 0:PW, PW:] - q_ref[i, PW:, 0:PW]
            if not begin:
                q_re += before_ref[k + i, 0]
                q_im += before_ref[k + i, 1]
            patch_ref[out, 0] = q_re
            patch_ref[out, 1] = q_im
            if final:
                send_ref[out, 0:PW] = q_re.astype(BF16)
                send_ref[out, PW : 2 * PW] = q_im.astype(BF16)

    if final:
        for i in range(per):
            column = jnp.sum(jnp.where(lane == k + i, listed, 0), axis=1, keepdims=True)
            column = jnp.where(k + i < total, column, EMPTY).astype(F32).astype(BF16)
            send_ref[i, 2 * PW :] = jnp.broadcast_to(column, (16, PW))
    if begin:

        @pl.when(step == pl.num_programs(0) - 1)
        def _():
            for copy in clears:
                copy.wait()


def residual(
    info, sources, capacity, first, steps, model_grid=None, kernels=None, tile_columns=0,
    prepared=None, before=None, final=False, unpacked=None, keep=False, per=1,
):
    begin = prepared is None
    slots = sources[0][0].shape[1]
    number = len(sources)
    in_vmem = pl.BlockSpec(memory_space=pltpu.VMEM)
    operands = [array for array, _ in sources] if unpacked is None else list(unpacked)
    in_specs = [in_vmem for _ in operands]
    out_specs = [in_vmem]
    out_shape = [jax.ShapeDtypeStruct((steps, 2, PW, PW), F32)]
    support, zeros, more = 0, 0, []
    if begin:
        support = kernels.shape[1] // 4
        width = min(tile_columns, 4 * PW)
        zeros = tile_columns // width
        patch_of = lambda s, i, j: (0, 0, jnp.maximum(i[0, jnp.minimum(s * per + j, capacity - 1)], 0))
        in_specs += [pl.BlockSpec((2, PW, PW), functools.partial(patch_of, j=j)) for j in range(per)]
        in_specs.append(whole_block(kernels.shape))
        operands += [in_hbm(model_grid)] * per + [in_hbm(kernels)]
        out_specs += [pl.BlockSpec(memory_space=pltpu.HBM), in_vmem, in_vmem]
        out_shape += [
            jax.ShapeDtypeStruct((2, PW, tile_columns), F32),
            jax.ShapeDtypeStruct((capacity, 2 * PW, 2 * PW), BF16),
            jax.ShapeDtypeStruct((4, 8, LANES), F32),
        ]
        more = [
            pltpu.VMEM((LANES, LANES), F32),
            pltpu.VMEM((2, PW, width), F32),
            pltpu.SemaphoreType.DMA((zeros,)),
        ]
    else:
        in_specs = [in_vmem] + in_specs + [in_vmem] * 3
        operands += [*prepared, before]
    if final:
        out_specs.append(in_vmem)
        out_shape.append(jax.ShapeDtypeStruct((steps, 2 * PW + 16, PW), BF16))
    fields = [((number * capacity, 8, slots), dtype) for dtype in (F32, I32)]
    scratch = [pltpu.VMEM((2 * PW, slots), BF16), pltpu.VMEM((per, 2 * PW, 2 * PW), F32)]
    if keep:
        out_specs += [in_vmem] * 2
        out_shape += [jax.ShapeDtypeStruct(*field) for field in fields]
    elif unpacked is None:
        scratch = [pltpu.VMEM(*field) for field in fields] + scratch
    scratch += [pltpu.VMEM((2 * PW, slots), BF16)] * number
    scratch += [pltpu.VMEM((2 * PW, slots), F32)] * number
    scratch += [pltpu.VMEM((2, 16, slots), F32)] * number
    scratch += [pltpu.VMEM((16, slots), I32)] * number
    return pl.pallas_call(
        functools.partial(
            residual_kernel, halves=tuple(half for _, half in sources), capacity=capacity, first=first,
            final=final, begin=begin, zeros=zeros, support=support, unpacked=unpacked is not None, keep=keep,
            per=per,
        ),
        grid_spec=pltpu.PrefetchScalarGridSpec(
            num_scalar_prefetch=1 if begin else 0, grid=(steps // per + 1 if begin else 1,), in_specs=in_specs, out_specs=out_specs,
            scratch_shapes=scratch + more,
        ),
        out_shape=out_shape,
        compiler_params=pltpu.CompilerParams(vmem_limit_bytes=VMEM_LIMIT),
        cost_estimate=pl.CostEstimate(
            flops=steps * number * slots * 16 * PW * PW, bytes_accessed=steps * 65536, transcendentals=0
        ),
        name="degrid_and_grid",
    )(info, *operands)


def place_own_kernel(info_ref, place_ref, *refs, groups, capacity, per_slab):
    own_refs = refs[:groups]
    tile_ref, sem = refs[groups + 1 :]
    slab_start = place_ref[1] * per_slab
    total = info_ref[0, capacity]
    slots = [ref.at[k] for ref in own_refs for k in range(ref.shape[0])]

    def each(act):
        for k in range(capacity):
            local = info_ref[0, k] - slab_start

            @pl.when((k < total) & (local >= 0) & (local < per_slab))
            def _():
                cols = pl.ds(pl.multiple_of(local * PW, PW), PW)
                act(pltpu.make_async_copy(slots[k], tile_ref.at[:, :, cols], sem.at[k]))

    each(lambda copy: copy.start())
    each(lambda copy: copy.wait())


def place_received_kernel(info_ref, place_ref, received_ref, *refs, groups, capacity, per_slab, reread):
    own_refs = refs[:groups]
    tile_ref, sum_ref, sem = refs[groups + 1 :]
    slab_start = place_ref[1] * per_slab
    total = info_ref[0, capacity]
    slots = [ref.at[k] for ref in own_refs for k in range(ref.shape[0])]
    number = received_ref.shape[0]
    columns = [jnp.max(received_ref[k, 2 * PW :].astype(F32)).astype(I32) for k in range(number)]

    def each(act):
        for k in range(number):
            local = columns[k] - slab_start

            @pl.when((local >= 0) & (local < per_slab))
            def _():
                cols = pl.ds(pl.multiple_of(local * PW, PW), PW)
                act(k, pltpu.make_async_copy(sum_ref.at[k], tile_ref.at[:, :, cols], sem.at[k]))

    def send(k, copy):
        if reread:
            cols = pl.ds(pl.multiple_of((columns[k] - slab_start) * PW, PW), PW)
            there = pltpu.make_async_copy(tile_ref.at[:, :, cols], sum_ref.at[k], sem.at[k])
            there.start()
            there.wait()
            sum_ref[k, 0] += received_ref[k, 0:PW].astype(F32)
            sum_ref[k, 1] += received_ref[k, PW : 2 * PW].astype(F32)
            copy.start()
            return
        sum_ref[k, 0] = received_ref[k, 0:PW].astype(F32)
        sum_ref[k, 1] = received_ref[k, PW : 2 * PW].astype(F32)
        for j in range(capacity):

            @pl.when((j < total) & (info_ref[0, j] == columns[k]))
            def _():
                sum_ref[k] += slots[j][...]

        copy.start()

    each(send)
    each(lambda k, copy: copy.wait())


def place_patches(kernel, info, place, received, own, tile, per_slab, reread=False):
    groups = len(own)
    capacity = sum(patches.shape[0] for patches in own)
    scratch = [pltpu.SemaphoreType.DMA((capacity,))]
    if received:
        number, _, width = received[0].shape
        scratch = [pltpu.VMEM((number, 2, tile.shape[1], PW), F32), pltpu.SemaphoreType.DMA((number,))]
        kernel = functools.partial(kernel, reread=reread)
    operands = [*received, *own]
    return pl.pallas_call(
        functools.partial(kernel, groups=groups, capacity=capacity, per_slab=per_slab),
        grid_spec=pltpu.PrefetchScalarGridSpec(
            num_scalar_prefetch=2,
            grid=(1,),
            in_specs=[pl.BlockSpec(memory_space=pltpu.VMEM)] * len(operands)
            + [pl.BlockSpec(memory_space=pltpu.HBM)],
            out_specs=pl.BlockSpec(memory_space=pltpu.HBM),
            scratch_shapes=scratch,
        ),
        out_shape=jax.ShapeDtypeStruct(tile.shape, tile.dtype),
        input_output_aliases={2 + len(operands): 0},
        compiler_params=pltpu.CompilerParams(vmem_limit_bytes=VMEM_LIMIT),
        name="place_received" if received else "place_own",
    )(info, place, *operands, tile)


def swap(array, axis, distance):
    size = lax.axis_size(axis)
    return lax.ppermute(array, axis, [(i, i ^ distance) for i in range(size)])


def shards(model_grid, kernels, cover, cells, planes, observed, weights):
    tiles = lax.axis_size("grid")
    slabs = lax.axis_size("vis")
    per_tile = model_grid.shape[2] // PW
    per_slab = per_tile // slabs
    capacity = 2 * cover.shape[1] // tiles
    place = jnp.stack([lax.axis_index("grid"), lax.axis_index("vis")]).astype(I32)
    lane = lax.broadcasted_iota(I32, (1, LANES), 1)
    places = jnp.where(lane == 0, place[0], place[1])
    info, *pairs = pack(places, cover, cells, planes, observed, weights, tiles, per_tile, per_slab)
    arrived = [swap(pairs[i], "grid", 2 * i) for i in reversed(range(1, tiles // 2))]
    arrived = [pairs[0]] + arrived[::-1]
    both = lambda pair: ((pair, 0), (swap(pair, "grid", 1), 1))
    near = both(arrived[1])
    early = both(arrived[0]) + near[:1]
    before, tile, *prepared = residual(
        info, early, capacity, 0, capacity, model_grid=model_grid, kernels=kernels,
        tile_columns=per_slab * PW, per=4,
    )
    run = functools.partial(residual, info, capacity=capacity, prepared=prepared)
    before, *rest = lax.optimization_barrier((before, *arrived[2:]))
    sources = near[1:] + sum((both(pair) for pair in rest), ())
    while len(sources) > 6:
        (before,) = run(sources[:4], first=0, steps=capacity, before=before, per=capacity)
        sources = sources[4:]
    own, received = [], []
    unpacked = None
    bounds = [part * capacity // 8 for part in (0, 3, 6, 8)]
    for first, end in zip(bounds, bounds[1:]):
        patches, send, *fields = run(
            sources, first=first, steps=end - first, before=before, final=True, unpacked=unpacked,
            keep=unpacked is None, per=end - first,
        )
        unpacked = unpacked or fields
        own.append(patches)
        received.append([swap(send, "vis", v) for v in range(1, slabs)])
    tile = place_patches(place_own_kernel, info, place, [], own, tile, per_slab)
    for group in received:
        for patches in group:
            tile = place_patches(place_received_kernel, info, place, [patches], own, tile, per_slab, slabs > 2)
    return tile


def solution(mesh):
    placed = (
        P("chan", "grid", None),
        P(),
        P(("chan", "vis"), None),
        P(("chan", "vis"), None, "grid"),
        P(("chan", "vis"), None, "grid"),
        P("chan", "vis", None, "grid"),
        P(("chan", "vis"), None, "grid"),
    )
    return jax.shard_map(
        shards, mesh=mesh, in_specs=placed, out_specs=P("chan", "grid", "vis"), check_vma=False
    )
```
